32 devices in a mesh: spec: 16 (over z, x, core), img: 2 (over y).
Axes of the slice: x: 2, y: 2, z: 4, core: 2. Of those that a mesh axis runs over, the one named last changes fastest.
Arguments:
- spec_emb: bfloat16 [2048, 1024], P('spec', 'img'), may hold values from -1024 to 1024
- img_emb: bfloat16 [512, 1024], P('img', 'spec'), may hold values from -16 to 16
- grad_spec: bfloat16 [2048, 1024], P('spec', 'img'), may hold values from -6 to 6
- grad_img: bfloat16 [512, 1024], P('img', 'spec'), may hold values from -6 to 6
Outputs:
- spec_emb_grad: bfloat16 [2048, 1024], P('spec', 'img')
- img_emb_grad: bfloat16 [512, 1024], P('img', 'spec')
The draws below stay inside these ranges and needn't reach their ends.
All inputs are finite; a program needn't handle non-finite values.
Results may differ from the reference program's by a relative error of at most 0.0109.
Values may be sent and summed in bfloat16 or wider, within the bound.
A program may use at most 64 MiB of HBM per device.

```python
import jax
import jax.numpy as jnp
from jax import lax

D = 1024
HEADS = 16
SPEC = 2048
IMG = 512


def drawn_pair(key):
    base = jax.random.fold_in(key, 4111)
    streams = jax.random.split(base, 2)
    image_rows = jax.random.truncated_normal(streams[0], -6.0, 6.0, (IMG, D), jnp.float32)
    spec_rows = jax.random.truncated_normal(streams[1], -6.0, 6.0, (SPEC, D), jnp.float32)
    return (spec_rows, image_rows)


def draw_spec_emb(key, part):
    return drawn_pair(key)[0].astype(jnp.bfloat16)


def draw_img_emb(key, part):
    return drawn_pair(key)[1].astype(jnp.bfloat16)


def levels(key, extent, cuts, low, high):
    level = 1.0
    for dim, shards_of in cuts:
        heights = jax.random.uniform(jax.random.fold_in(jax.random.fold_in(key, 6), dim), (shards_of,), jnp.float32, low / len(cuts), high / len(cuts))
        level = level * jnp.repeat(jnp.exp(heights), extent[dim] // shards_of).reshape((-1,) + (1,) * (len(extent) - 1 - dim))
    return level


def scatter_about(own_key, extent, spread, most, cuts=(), dtype=jnp.bfloat16):
    level = levels(own_key, extent, cuts, -0.22, 0.18) if cuts else 1.0
    drawn = jax.random.normal(own_key, extent, jnp.float32) * spread * level
    return jnp.minimum(jnp.maximum(drawn, -most), most).astype(dtype)


def setup_inputs(seed: int = 0) -> dict:
    key_list = jax.random.split(jax.random.key(seed), 5)
    return {
        "spec_emb": draw_spec_emb(jax.random.fold_in(key_list[4], 71), 0),
        "img_emb": draw_img_emb(jax.random.fold_in(key_list[4], 71), 0),
        "grad_spec": scatter_about(key_list[2], (SPEC, D), 1.0, 6.0, ((0, 16), (1, 2))),
        "grad_img": scatter_about(key_list[3], (IMG, D), 1.0, 6.0, ((0, 2), (1, 16))),
    }


def head_terms(operands):
    spec_rows, spec_grad, image_rows, image_grad = operands
    scale = (D // HEADS) ** -0.5
    scores = jnp.dot(spec_rows, image_rows.T, preferred_element_type=jnp.float32) * scale
    row_moment = jnp.dot(spec_grad, image_rows.T, preferred_element_type=jnp.float32)
    column_moment = jnp.dot(spec_rows, image_grad.T, preferred_element_type=jnp.float32)
    row_scaled = jnp.exp(scores - jnp.max(scores, axis=1, keepdims=True))
    row_weight = row_scaled / jnp.sum(row_scaled, axis=1, keepdims=True)
    column_scaled = jnp.exp(scores - jnp.max(scores, axis=0, keepdims=True))
    column_weight = column_scaled / jnp.sum(column_scaled, axis=0, keepdims=True)
    row_delta = jnp.sum(row_weight * row_moment, axis=1, keepdims=True)
    column_delta = jnp.sum(column_weight * column_moment, axis=0, keepdims=True)
    slope = (row_weight * (row_moment - row_delta) + column_weight * (column_moment - column_delta)).astype(jnp.bfloat16)
    spec_part = scale * jnp.dot(slope, image_rows, preferred_element_type=jnp.float32) + jnp.dot(column_weight.astype(jnp.bfloat16), image_grad, preferred_element_type=jnp.float32)
    image_part = scale * jnp.dot(slope.T, spec_rows, preferred_element_type=jnp.float32) + jnp.dot(row_weight.astype(jnp.bfloat16).T, spec_grad, preferred_element_type=jnp.float32)
    return spec_part, image_part


def by_heads(array):
    return jnp.transpose(array.reshape(array.shape[0], HEADS, D // HEADS), (1, 0, 2))


def joined(array):
    return jnp.transpose(array, (1, 0, 2)).reshape(array.shape[1], D)


def reference(spec_emb, img_emb, grad_spec, grad_img):
    spec_parts, image_parts = lax.map(head_terms, (by_heads(spec_emb), by_heads(grad_spec), by_heads(img_emb), by_heads(grad_img)))
    return joined(spec_parts).astype(jnp.bfloat16), joined(image_parts).astype(jnp.bfloat16)
```

```python
import functools

import jax
import jax.numpy as jnp
from jax import lax
from jax.experimental import pallas as pl
from jax.experimental.pallas import tpu as pltpu
from jax.sharding import PartitionSpec as P

D = 1024
HEADS = 16
GROUP = 4


def row_totals(scores, moment):
    highest = lax.pmax(jnp.max(scores, axis=2, keepdims=True), "img")
    scaled = jnp.exp(scores - highest)
    total = lax.psum(jnp.sum(scaled, axis=2, keepdims=True), "img")
    weights = scaled / total
    delta = lax.psum(jnp.sum(weights * moment, axis=2, keepdims=True), "img")
    return (weights, delta)


def column_totals(scores, moment):
    highest = lax.pmax(jnp.max(scores, axis=1, keepdims=True), "spec")
    scaled = jnp.exp(scores - highest)
    total = lax.psum(jnp.sum(scaled, axis=1, keepdims=True), "spec")
    weights = scaled / total
    delta = lax.psum(jnp.sum(weights * moment, axis=1, keepdims=True), "spec")
    return (weights, delta)


def score_block(spec_rows, spec_grad, image_rows, image_grad, row_rule, column_rule):
    scale = (D // HEADS) ** (-0.5)
    scores = (
        jnp.einsum("shd,ihd->hsi", spec_rows, image_rows, preferred_element_type=jnp.float32)
        * scale
    )
    row_moment = jnp.einsum(
        "shd,ihd->hsi", spec_grad, image_rows, preferred_element_type=jnp.float32
    )
    column_moment = jnp.einsum(
        "shd,ihd->hsi", spec_rows, image_grad, preferred_element_type=jnp.float32
    )
    row_weight, row_delta = row_rule(scores, row_moment)
    column_weight, column_delta = column_rule(scores, column_moment)
    slope = (
        row_weight * (row_moment - row_delta) + column_weight * (column_moment - column_delta)
    ).astype(jnp.bfloat16)
    spec_part = scale * jnp.einsum(
        "hsi,ihd->shd", slope, image_rows, preferred_element_type=jnp.float32
    )
    spec_part = spec_part + jnp.einsum(
        "hsi,ihd->shd",
        column_weight.astype(jnp.bfloat16),
        image_grad,
        preferred_element_type=jnp.float32,
    )
    image_part = scale * jnp.einsum(
        "hsi,shd->ihd", slope, spec_rows, preferred_element_type=jnp.float32
    )
    image_part = image_part + jnp.einsum(
        "hsi,shd->ihd",
        row_weight.astype(jnp.bfloat16),
        spec_grad,
        preferred_element_type=jnp.float32,
    )
    return (spec_part, image_part)


def shards(spec_emb, img_emb, grad_spec, grad_img):
    head_size = D // HEADS
    spec_count = spec_emb.shape[0]
    spec_all, spec_grad_all = (
        lax.all_gather(spec_emb, "img", axis=1, tiled=True),
        lax.all_gather(grad_spec, "img", axis=1, tiled=True),
    )
    image_all, image_grad_all = (
        lax.all_gather(img_emb, "spec", axis=1, tiled=True),
        lax.all_gather(grad_img, "spec", axis=1, tiled=True),
    )
    image_count = image_all.shape[0]
    spec_heads = spec_all.reshape(spec_count, HEADS, head_size)
    spec_grad_heads = spec_grad_all.reshape(spec_count, HEADS, head_size)
    image_heads = image_all.reshape(image_count, HEADS, head_size)
    image_grad_heads = image_grad_all.reshape(image_count, HEADS, head_size)
    spec_parts = []
    image_parts = []
    for block_index in range(HEADS // GROUP):
        window = slice(block_index * GROUP, (block_index + 1) * GROUP)
        spec_part, image_part = score_block(
            spec_heads[:, window],
            spec_grad_heads[:, window],
            image_heads[:, window],
            image_grad_heads[:, window],
            row_totals,
            column_totals,
        )
        spec_parts.append(spec_part)
        image_parts.append(image_part)
    spec_total = jnp.concatenate(spec_parts, axis=1).reshape(spec_count, D)
    image_total = jnp.concatenate(image_parts, axis=1).reshape(image_count, D)
    spec_result = lax.psum_scatter(
        spec_total.astype(jnp.bfloat16), "img", scatter_dimension=1, tiled=True
    )
    image_result = lax.psum_scatter(image_total, "spec", scatter_dimension=1, tiled=True).astype(
        jnp.bfloat16
    )
    return (spec_result, image_result)


F32 = jnp.float32
BF16 = jnp.bfloat16
NT = (((1,), (1,)), ((), ()))
TN = (((0,), (0,)), ((), ()))
NN = (((1,), (0,)), ((), ()))


def dot(a, b, dims):
    return lax.dot_general(a, b, dims, preferred_element_type=F32)


def head_kernel(
    chips, scale,
    spec_emb, img_emb, grad_spec, grad_img, spec_out, img_out,
    x_send, x, y_send, y, w, z, p, q, s16, c16, acc,
    stat_send, stat, part, part_in, o_send, o, g_send, g,
    xs_sem, xr_sem, ys_sem, yr_sem, os_sem, or_sem, pair_send, pair_recv, gs_sem, gr_sem,
):
    rows = spec_emb.shape[0]
    half = rows // 2
    size = img_emb.shape[1]
    cols = y.shape[1]
    images = 2 * cols
    me_s, me_i = lax.axis_index("spec"), lax.axis_index("img")
    chip, core = me_s // 2, me_s % 2
    mine = me_i * chips + chip
    to_s, to_i = 2 * (me_s % chips), me_s // chips
    is_self = (to_s + me_i == me_s) & (to_i == me_i)

    def remote(src, dst, send, recv, s, i):
        return pltpu.make_async_remote_copy(
            src_ref=src, dst_ref=dst, send_sem=send, recv_sem=recv,
            device_id={"spec": s, "img": i}, device_id_type=pl.DeviceIdType.MESH,
        )

    barrier = pltpu.get_barrier_semaphore()

    def greet(s, i):
        pl.semaphore_signal(
            barrier, inc=1, device_id={"spec": s, "img": i}, device_id_type=pl.DeviceIdType.MESH
        )

    for t in range(1, chips):
        greet(2 * lax.rem(chip + t, chips) + core, me_i)
    sibling = 2 * chip + 1 - core
    greet(sibling, me_i)
    for i in range(2):
        own = (mine == me_s) & (me_i == i)

        @pl.when(jnp.logical_not(own))
        def _():
            greet(mine, i)

    @pl.when(jnp.logical_not(is_self))
    def _():
        greet(to_s + me_i, to_i)

    y_send[...] = jnp.concatenate([img_emb[...], grad_img[...]], axis=1)
    for j in range(chips):
        part_of = slice(j * size, (j + 1) * size)
        x_send[j] = jnp.concatenate([spec_emb[:, part_of], grad_spec[:, part_of]], axis=1)

    @pl.when(is_self)
    def _():
        pl.semaphore_wait(barrier, chips + 1)

    @pl.when(jnp.logical_not(is_self))
    def _():
        pl.semaphore_wait(barrier, chips + 3)

    def image_copy(cc):
        return remote(y_send, y.at[me_i], ys_sem.at[cc], yr_sem.at[me_i], to_s + cc, to_i)

    for cc in range(2):
        own = (to_s + cc == me_s) & (to_i == me_i)

        @pl.when(jnp.logical_not(own))
        def _():
            image_copy(cc).start()

        @pl.when(own)
        def _():
            y[me_i] = y_send[...]

    def x_copy(j):
        return remote(
            x_send.at[j], x.at[chip], xs_sem.at[j], xr_sem.at[chip], 2 * j + core, me_i
        )

    for t in range(1, chips):
        x_copy(lax.rem(chip + t, chips)).start()
    x[chip] = x_send[chip]

    for i in range(2):
        own = (mine == me_s) & (me_i == i)

        @pl.when(jnp.logical_not(own))
        def _():
            remote(y_send, y.at[i], ys_sem.at[0], yr_sem.at[i], mine, i).wait_recv()

        both = y[i]
        e, d = both[:, :size], both[:, size:]
        zero = jnp.zeros_like(e)
        w[pl.ds(i * cols, cols)] = jnp.concatenate([e, zero], axis=1)
        w[pl.ds(images + i * cols, cols)] = jnp.concatenate([zero, e], axis=1)
        w[pl.ds(2 * images + i * cols, cols)] = jnp.concatenate([d, zero], axis=1)

    def arrive(t, carry):
        top, total, moment = carry
        j = lax.rem(chip + chips - t, chips)

        @pl.when(t > 0)
        def _():
            remote(
                x_send.at[j], x.at[j], xs_sem.at[j], xr_sem.at[j], 2 * j + core, me_i
            ).wait_recv()

        all3 = dot(x[j], w[...], NT)
        zj = all3[:, :images] * scale
        qj = all3[:, 2 * images :]
        z[j] = zj
        p[j] = all3[:, images : 2 * images]
        q[j] = qj
        new = jnp.maximum(top, jnp.max(zj, axis=0, keepdims=True))
        fade = jnp.exp(top - new)
        e = jnp.exp(zj - new)
        total = total * fade + jnp.sum(e, axis=0, keepdims=True)
        moment = moment * fade + jnp.sum(e * qj, axis=0, keepdims=True)
        return new, total, moment

    start = jnp.full((1, images), -jnp.inf, F32)
    nothing = jnp.zeros((1, images), F32)
    top, total, moment = lax.fori_loop(0, chips, arrive, (start, nothing, nothing))
    stat_send[0:1] = top
    stat_send[1:2] = total
    stat_send[2:3] = moment
    stat_copy = remote(stat_send, stat, pair_send.at[0], pair_recv.at[0], sibling, me_i)
    stat_copy.start()

    acc[...] = jnp.zeros_like(acc)

    def by_row(j, carry):
        zj, pj = z[j], p[j]
        e = jnp.exp(zj - jnp.max(zj, axis=1, keepdims=True))
        weight = e * (1.0 / jnp.sum(e, axis=1, keepdims=True))
        delta = jnp.sum(weight * pj, axis=1, keepdims=True)
        p[j] = weight * (pj - delta)
        acc[...] += dot(x[j], weight.astype(BF16), TN)[size:]
        return carry

    lax.fori_loop(0, chips, by_row, 0)

    stat_copy.wait()
    other = stat[0:1]
    high = jnp.maximum(top, other)
    here, there = jnp.exp(top - high), jnp.exp(other - high)
    inverse = 1.0 / (total * here + stat[1:2] * there)
    column_delta = (moment * here + stat[2:3] * there) * inverse

    def by_column(j, carry):
        weight = jnp.exp(z[j] - high) * inverse
        slope = (p[j] + weight * (q[j] - column_delta)).astype(BF16)
        s16[j] = slope
        c16[j] = weight.astype(BF16)
        acc[...] += scale * dot(x[j], slope, TN)[:size]
        return carry

    lax.fori_loop(0, chips, by_column, 0)
    for i in range(2):
        part[i] = acc[:, i * cols : (i + 1) * cols]
    part_copy = remote(part.at[1 - core], part_in, pair_send.at[1], pair_recv.at[1], sibling, me_i)
    part_copy.start()

    def o_copy(j):
        return remote(
            o_send.at[j], o.at[chip], os_sem.at[j], or_sem.at[chip], 2 * j + core, me_i
        )

    features = jnp.concatenate([y[0], y[1]], axis=0)

    def spec_rows(t, carry):
        j = lax.rem(chip + t, chips)
        value = scale * dot(s16[j], features, NN)[:, :size] + dot(c16[j], features, NN)[:, size:]
        o_send[j] = jnp.concatenate([value[:half], value[half:]], axis=1).astype(BF16)
        o_copy(j).start()
        return carry

    lax.fori_loop(1, chips, spec_rows, 0)
    part_copy.wait()
    g_send[...] = (part[core] + part_in[...]).astype(BF16)
    g_copy = remote(g_send, g, gs_sem, gr_sem, mine, core)

    out_self = (mine == me_s) & (core == me_i)

    @pl.when(jnp.logical_not(out_self))
    def _():
        g_copy.start()

    @pl.when(out_self)
    def _():
        g[...] = g_send[...]

    value = scale * dot(s16[chip], features, NN)[:, :size] + dot(c16[chip], features, NN)[:, size:]
    o[chip] = jnp.concatenate([value[:half], value[half:]], axis=1).astype(BF16)

    for t in range(1, chips):
        j = lax.rem(chip + chips - t, chips)
        remote(o_send.at[j], o.at[j], os_sem.at[j], or_sem.at[j], 2 * j + core, me_i).wait_recv()
    for a in range(chips // 2):
        b0, b1 = o[2 * a], o[2 * a + 1]
        spec_out[:half, 2 * a * size : 2 * (a + 1) * size] = jnp.concatenate(
            [b0[:, :size], b1[:, :size]], axis=1
        )
        spec_out[half:, 2 * a * size : 2 * (a + 1) * size] = jnp.concatenate(
            [b0[:, size:], b1[:, size:]], axis=1
        )

    @pl.when(jnp.logical_not(is_self))
    def _():
        remote(g_send, g, gs_sem, gr_sem, to_s + me_i, to_i).wait_recv()

    img_out[...] = g[...].astype(F32).T.astype(BF16)

    for t in range(1, chips):
        j = lax.rem(chip + t, chips)
        x_copy(j).wait_send()
        o_copy(j).wait_send()
    for cc in range(2):
        own = (to_s + cc == me_s) & (to_i == me_i)

        @pl.when(jnp.logical_not(own))
        def _():
            image_copy(cc).wait_send()

    @pl.when(jnp.logical_not(out_self))
    def _():
        g_copy.wait_send()


def head_shards(chips, spec_emb, img_emb, grad_spec, grad_img):
    rows, width = spec_emb.shape
    cols, size = img_emb.shape
    images = 2 * cols
    vmem, dma = pltpu.VMEM, pltpu.SemaphoreType.DMA
    return pl.pallas_call(
        functools.partial(head_kernel, chips, size**-0.5),
        out_shape=(
            jax.ShapeDtypeStruct((rows, width), BF16),
            jax.ShapeDtypeStruct((cols, size), BF16),
        ),
        in_specs=[pl.BlockSpec(memory_space=vmem)] * 4,
        out_specs=[pl.BlockSpec(memory_space=vmem)] * 2,
        scratch_shapes=[
            vmem((chips, rows, 2 * size), BF16),
            vmem((chips, rows, 2 * size), BF16),
            vmem((cols, 2 * size), BF16),
            vmem((2, cols, 2 * size), BF16),
            vmem((3 * images, 2 * size), BF16),
            vmem((chips, rows, images), F32),
            vmem((chips, rows, images), F32),
            vmem((chips, rows, images), F32),
            vmem((chips, rows, images), BF16),
            vmem((chips, rows, images), BF16),
            vmem((size, images), F32),
            vmem((8, images), F32),
            vmem((8, images), F32),
            vmem((2, size, cols), F32),
            vmem((size, cols), F32),
            vmem((chips, rows // 2, 2 * size), BF16),
            vmem((chips, rows // 2, 2 * size), BF16),
            vmem((size, cols), BF16),
            vmem((size, cols), BF16),
            dma((chips,)), dma((chips,)), dma((2,)), dma((2,)),
            dma((chips,)), dma((chips,)), dma((2,)), dma((2,)), dma, dma,
        ],
        compiler_params=pltpu.CompilerParams(
            collective_id=0, has_side_effects=True, vmem_limit_bytes=40 * 2**20
        ),
    )(spec_emb, img_emb, grad_spec, grad_img)


def solution(mesh):
    in_specs = (P("spec", "img"), P("img", "spec"), P("spec", "img"), P("img", "spec"))
    out_specs = (P("spec", "img"), P("img", "spec"))
    chips = mesh.shape["spec"] // 2
    body = shards
    if mesh.shape["spec"] == HEADS and mesh.shape["img"] == 2 and chips % 2 == 0:
        body = functools.partial(head_shards, chips)
    return jax.shard_map(body, mesh=mesh, in_specs=in_specs, out_specs=out_specs, check_vma=False)
```

```python
import functools

import jax
import jax.numpy as jnp
from jax import lax
from jax.experimental import pallas as pl
from jax.experimental.pallas import tpu as pltpu
from jax.sharding import PartitionSpec as P

D = 1024
HEADS = 16
GROUP = 4


def row_totals(scores, moment):
    highest = lax.pmax(jnp.max(scores, axis=2, keepdims=True), "img")
    scaled = jnp.exp(scores - highest)
    total = lax.psum(jnp.sum(scaled, axis=2, keepdims=True), "img")
    weights = scaled / total
    delta = lax.psum(jnp.sum(weights * moment, axis=2, keepdims=True), "img")
    return (weights, delta)


def column_totals(scores, moment):
    highest = lax.pmax(jnp.max(scores, axis=1, keepdims=True), "spec")
    scaled = jnp.exp(scores - highest)
    total = lax.psum(jnp.sum(scaled, axis=1, keepdims=True), "spec")
    weights = scaled / total
    delta = lax.psum(jnp.sum(weights * moment, axis=1, keepdims=True), "spec")
    return (weights, delta)


def score_block(spec_rows, spec_grad, image_rows, image_grad, row_rule, column_rule):
    scale = (D // HEADS) ** (-0.5)
    scores = (
        jnp.einsum("shd,ihd->hsi", spec_rows, image_rows, preferred_element_type=jnp.float32)
        * scale
    )
    row_moment = jnp.einsum(
        "shd,ihd->hsi", spec_grad, image_rows, preferred_element_type=jnp.float32
    )
    column_moment = jnp.einsum(
        "shd,ihd->hsi", spec_rows, image_grad, preferred_element_type=jnp.float32
    )
    row_weight, row_delta = row_rule(scores, row_moment)
    column_weight, column_delta = column_rule(scores, column_moment)
    slope = (
        row_weight * (row_moment - row_delta) + column_weight * (column_moment - column_delta)
    ).astype(jnp.bfloat16)
    spec_part = scale * jnp.einsum(
        "hsi,ihd->shd", slope, image_rows, preferred_element_type=jnp.float32
    )
    spec_part = spec_part + jnp.einsum(
        "hsi,ihd->shd",
        column_weight.astype(jnp.bfloat16),
        image_grad,
        preferred_element_type=jnp.float32,
    )
    image_part = scale * jnp.einsum(
        "hsi,shd->ihd", slope, spec_rows, preferred_element_type=jnp.float32
    )
    image_part = image_part + jnp.einsum(
        "hsi,shd->ihd",
        row_weight.astype(jnp.bfloat16),
        spec_grad,
        preferred_element_type=jnp.float32,
    )
    return (spec_part, image_part)


def shards(spec_emb, img_emb, grad_spec, grad_img):
    head_size = D // HEADS
    spec_count = spec_emb.shape[0]
    spec_all, spec_grad_all = (
        lax.all_gather(spec_emb, "img", axis=1, tiled=True),
        lax.all_gather(grad_spec, "img", axis=1, tiled=True),
    )
    image_all, image_grad_all = (
        lax.all_gather(img_emb, "spec", axis=1, tiled=True),
        lax.all_gather(grad_img, "spec", axis=1, tiled=True),
    )
    image_count = image_all.shape[0]
    spec_heads = spec_all.reshape(spec_count, HEADS, head_size)
    spec_grad_heads = spec_grad_all.reshape(spec_count, HEADS, head_size)
    image_heads = image_all.reshape(image_count, HEADS, head_size)
    image_grad_heads = image_grad_all.reshape(image_count, HEADS, head_size)
    spec_parts = []
    image_parts = []
    for block_index in range(HEADS // GROUP):
        window = slice(block_index * GROUP, (block_index + 1) * GROUP)
        spec_part, image_part = score_block(
            spec_heads[:, window],
            spec_grad_heads[:, window],
            image_heads[:, window],
            image_grad_heads[:, window],
            row_totals,
            column_totals,
        )
        spec_parts.append(spec_part)
        image_parts.append(image_part)
    spec_total = jnp.concatenate(spec_parts, axis=1).reshape(spec_count, D)
    image_total = jnp.concatenate(image_parts, axis=1).reshape(image_count, D)
    spec_result = lax.psum_scatter(
        spec_total.astype(jnp.bfloat16), "img", scatter_dimension=1, tiled=True
    )
    image_result = lax.psum_scatter(image_total, "spec", scatter_dimension=1, tiled=True).astype(
        jnp.bfloat16
    )
    return (spec_result, image_result)


F32 = jnp.float32
BF16 = jnp.bfloat16
NT = (((1,), (1,)), ((), ()))
TN = (((0,), (0,)), ((), ()))
NN = (((1,), (0,)), ((), ()))


def dot(a, b, dims):
    return lax.dot_general(a, b, dims, preferred_element_type=F32)


def head_kernel(
    chips, scale,
    spec_emb_in, img_emb_in, grad_spec_in, grad_img_in, spec_out, img_out,
    x_send, x, y_send, y, w, z, p, q, acc,
    stat_send, stat, part, part_in, o_send, o, g_send, g,
    xs_sem, xr_sem, ys_sem, yr_sem, os_sem, or_sem, pair_send, pair_recv, gs_sem, gr_sem,
    spec_emb, grad_spec, load_sem, features,
):
    rows = spec_emb_in.shape[0]
    half = rows // 2
    size, cols = img_emb_in.shape
    images = 2 * cols
    me_s, me_i = lax.axis_index("spec"), lax.axis_index("img")
    chip, core = me_s // 2, me_s % 2
    mine = me_i * chips + chip
    to_s, to_i = 2 * (me_s % chips), me_s // chips
    is_self = (to_s + me_i == me_s) & (to_i == me_i)

    def remote(src, dst, send, recv, s, i):
        return pltpu.make_async_remote_copy(
            src_ref=src, dst_ref=dst, send_sem=send, recv_sem=recv,
            device_id={"spec": s, "img": i}, device_id_type=pl.DeviceIdType.MESH,
        )

    loads = [
        pltpu.make_async_copy(src, dst, load_sem.at[n])
        for n, (src, dst) in enumerate(
            (
                (img_emb_in, y_send.at[pl.ds(0, size)]),
                (grad_img_in, y_send.at[pl.ds(size, size)]),
                (spec_emb_in, spec_emb),
                (grad_spec_in, grad_spec),
            )
        )
    ]
    barrier = pltpu.get_barrier_semaphore()

    def greet(s, i):
        pl.semaphore_signal(
            barrier, inc=1, device_id={"spec": s, "img": i}, device_id_type=pl.DeviceIdType.MESH
        )

    for t in range(1, chips):
        greet(2 * lax.rem(chip + t, chips) + core, me_i)
    sibling = 2 * chip + 1 - core
    greet(sibling, me_i)
    for i in range(2):
        own = (mine == me_s) & (me_i == i)

        @pl.when(jnp.logical_not(own))
        def _():
            greet(mine, i)

    @pl.when(jnp.logical_not(is_self))
    def _():
        greet(to_s + me_i, to_i)

    for load in loads:
        load.start()
    for load in loads:
        load.wait()
    for j in range(chips):
        part_of = slice(j * size, (j + 1) * size)
        x_send[j] = jnp.concatenate([spec_emb[:, part_of], grad_spec[:, part_of]], axis=1)

    @pl.when(is_self)
    def _():
        pl.semaphore_wait(barrier, chips + 1)

    @pl.when(jnp.logical_not(is_self))
    def _():
        pl.semaphore_wait(barrier, chips + 3)

    def image_copy(cc):
        return remote(y_send, y.at[me_i], ys_sem.at[cc], yr_sem.at[me_i], to_s + cc, to_i)

    for cc in range(2):
        own = (to_s + cc == me_s) & (to_i == me_i)

        @pl.when(jnp.logical_not(own))
        def _():
            image_copy(cc).start()

        @pl.when(own)
        def _():
            y[me_i] = y_send[...]

    def x_copy(j):
        return remote(
            x_send.at[j], x.at[chip], xs_sem.at[j], xr_sem.at[chip], 2 * j + core, me_i
        )

    for t in range(1, chips):
        x_copy(lax.rem(chip + t, chips)).start()
    x[chip] = x_send[chip]

    for i in range(2):
        own = (mine == me_s) & (me_i == i)

        @pl.when(jnp.logical_not(own))
        def _():
            remote(y_send, y.at[i], ys_sem.at[0], yr_sem.at[i], mine, i).wait_recv()

        e, d = y[i, :size], y[i, size:]
        zero = jnp.zeros_like(e)
        for n, pair in enumerate(((e, zero), (zero, e), (d, zero))):
            w[:size, n * images + i * cols : n * images + (i + 1) * cols] = pair[0]
            w[size:, n * images + i * cols : n * images + (i + 1) * cols] = pair[1]

    acc[...] = jnp.zeros_like(acc)

    def by_row(j, zj, pj):
        e = jnp.exp(zj - jnp.max(zj, axis=1, keepdims=True))
        weight = e * (1.0 / jnp.sum(e, axis=1, keepdims=True))
        delta = jnp.sum(weight * pj, axis=1, keepdims=True)
        p[j] = weight * (pj - delta)
        acc[...] += dot(x[j], weight.astype(BF16), TN)[size:]

    def arrive(with_rows, t, carry):
        top, total, moment = carry
        j = lax.rem(chip + chips - t, chips)

        @pl.when(t > 0)
        def _():
            remote(
                x_send.at[j], x.at[j], xs_sem.at[j], xr_sem.at[j], 2 * j + core, me_i
            ).wait_recv()

        all3 = dot(x[j], w[...], NN)
        zj = all3[:, :images] * scale
        qj = all3[:, 2 * images :]
        z[j] = zj
        pj = all3[:, images : 2 * images]
        if with_rows:
            by_row(j, zj, pj)
        else:
            p[j] = pj
        q[j] = qj
        new = jnp.maximum(top, jnp.max(zj, axis=0, keepdims=True))
        fade = jnp.exp(top - new)
        e = jnp.exp(zj - new)
        total = total * fade + jnp.sum(e, axis=0, keepdims=True)
        moment = moment * fade + jnp.sum(e * qj, axis=0, keepdims=True)
        return new, total, moment

    start = jnp.full((1, images), -jnp.inf, F32)
    nothing = jnp.zeros((1, images), F32)
    early = chips // 2
    sums = lax.fori_loop(0, early, functools.partial(arrive, True), (start, nothing, nothing))
    top, total, moment = lax.fori_loop(early, chips, functools.partial(arrive, False), sums)
    stat_send[0:1] = top
    stat_send[1:2] = total
    stat_send[2:3] = moment
    stat_copy = remote(stat_send, stat, pair_send.at[0], pair_recv.at[0], sibling, me_i)
    stat_copy.start()

    def late(t, carry):
        j = lax.rem(chip + chips - t, chips)
        by_row(j, z[j], p[j])
        return carry

    lax.fori_loop(early, chips, late, 0, unroll=2)

    for i in range(2):
        features[pl.ds(i * cols, cols)] = y[i].T
    stat_copy.wait()
    other = stat[0:1]
    high = jnp.maximum(top, other)
    here, there = jnp.exp(top - high), jnp.exp(other - high)
    inverse = 1.0 / (total * here + stat[1:2] * there)
    column_delta = (moment * here + stat[2:3] * there) * inverse

    def o_copy(j):
        return remote(
            o_send.at[j], o.at[chip], os_sem.at[j], or_sem.at[chip], 2 * j + core, me_i
        )

    def by_column(t, carry):
        j = lax.rem(chip + t, chips)
        weight = jnp.exp(z[j] - high) * inverse
        slope = (p[j] + weight * (q[j] - column_delta)).astype(BF16)
        acc[...] += scale * dot(x[j], slope, TN)[:size]
        value = scale * dot(slope, features[...], NN)[:, :size]
        value += dot(weight.astype(BF16), features[...], NN)[:, size:]
        o_send[j] = jnp.concatenate([value[:half], value[half:]], axis=1).astype(BF16)

        @pl.when(t < chips)
        def _():
            o_copy(j).start()

        return carry

    lax.fori_loop(1, chips + 1, by_column, 0, unroll=2)
    for i in range(2):
        part[i] = acc[:, i * cols : (i + 1) * cols]
    part_copy = remote(part.at[1 - core], part_in, pair_send.at[1], pair_recv.at[1], sibling, me_i)
    part_copy.start()

    part_copy.wait()
    g_send[...] = (part[core] + part_in[...]).astype(BF16)
    g_copy = remote(g_send, g, gs_sem, gr_sem, mine, core)

    out_self = (mine == me_s) & (core == me_i)

    @pl.when(jnp.logical_not(out_self))
    def _():
        g_copy.start()

    @pl.when(out_self)
    def _():
        g[...] = g_send[...]

    o[chip] = o_send[chip]

    for t in range(1, chips):
        j = lax.rem(chip + chips - t, chips)
        remote(o_send.at[j], o.at[j], os_sem.at[j], or_sem.at[j], 2 * j + core, me_i).wait_recv()
    for a in range(chips // 2):
        b0, b1 = o[2 * a], o[2 * a + 1]
        spec_out[:half, 2 * a * size : 2 * (a + 1) * size] = jnp.concatenate(
            [b0[:, :size], b1[:, :size]], axis=1
        )
        spec_out[half:, 2 * a * size : 2 * (a + 1) * size] = jnp.concatenate(
            [b0[:, size:], b1[:, size:]], axis=1
        )

    @pl.when(jnp.logical_not(is_self))
    def _():
        remote(g_send, g, gs_sem, gr_sem, to_s + me_i, to_i).wait_recv()

    img_out[...] = g[...]

    for t in range(1, chips):
        j = lax.rem(chip + t, chips)
        x_copy(j).wait_send()
        o_copy(j).wait_send()
    for cc in range(2):
        own = (to_s + cc == me_s) & (to_i == me_i)

        @pl.when(jnp.logical_not(own))
        def _():
            image_copy(cc).wait_send()

    @pl.when(jnp.logical_not(out_self))
    def _():
        g_copy.wait_send()


def head_shards(chips, spec_emb, img_emb, grad_spec, grad_img):
    rows, width = spec_emb.shape
    cols, size = img_emb.shape
    images = 2 * cols
    vmem, dma = pltpu.VMEM, pltpu.SemaphoreType.DMA
    spec_grad, img_grad = pl.pallas_call(
        functools.partial(head_kernel, chips, size**-0.5),
        out_shape=(
            jax.ShapeDtypeStruct((rows, width), BF16),
            jax.ShapeDtypeStruct((size, cols), BF16),
        ),
        in_specs=[pl.BlockSpec(memory_space=pltpu.HBM)] * 4,
        out_specs=[pl.BlockSpec(memory_space=vmem)] * 2,
        scratch_shapes=[
            vmem((chips, rows, 2 * size), BF16),
            vmem((chips, rows, 2 * size), BF16),
            vmem((2 * size, cols), BF16),
            vmem((2, 2 * size, cols), BF16),
            vmem((2 * size, 3 * images), BF16),
            vmem((chips, rows, images), F32),
            vmem((chips, rows, images), F32),
            vmem((chips, rows, images), F32),
            vmem((size, images), F32),
            vmem((8, images), F32),
            vmem((8, images), F32),
            vmem((2, size, cols), F32),
            vmem((size, cols), F32),
            vmem((chips, rows // 2, 2 * size), BF16),
            vmem((chips, rows // 2, 2 * size), BF16),
            vmem((size, cols), BF16),
            vmem((size, cols), BF16),
            dma((chips,)), dma((chips,)), dma((2,)), dma((2,)),
            dma((chips,)), dma((chips,)), dma((2,)), dma((2,)), dma, dma,
            vmem((rows, width), BF16), vmem((rows, width), BF16), dma((4,)),
            vmem((images, 2 * size), BF16),
        ],
        compiler_params=pltpu.CompilerParams(
            collective_id=0, has_side_effects=True, vmem_limit_bytes=40 * 2**20
        ),
    )(spec_emb, img_emb.T, grad_spec, grad_img.T)
    return spec_grad, img_grad.T


def solution(mesh):
    in_specs = (P("spec", "img"), P("img", "spec"), P("spec", "img"), P("img", "spec"))
    out_specs = (P("spec", "img"), P("img", "spec"))
    chips = mesh.shape["spec"] // 2
    body = shards
    if mesh.shape["spec"] == HEADS and mesh.shape["img"] == 2 and chips % 2 == 0:
        body = functools.partial(head_shards, chips)
    return jax.shard_map(body, mesh=mesh, in_specs=in_specs, out_specs=out_specs, check_vma=False)
```
